256 devices in a mesh: track: 16 (over y, z_hi), rep: 16 (over x, z_lo, core).
Axes of the slice: x: 4, y: 4, z: 8 (z_hi: 4, z_lo: 2; z = z_hi * 2 + z_lo), core: 2. Of those that a mesh axis runs over, the one named last changes fastest.
Arguments:
- features: bfloat16 [16, 32, 32, 2048], P('rep', None, None, 'track'), may hold values from -6 to 6
- kernel_one: bfloat16 [5, 5, 32, 128], replicated, may hold values from -0.21875 to 0.21875
- kernel_two: bfloat16 [3, 3, 128, 128], replicated, may hold values from -0.1875 to 0.1875
- cotangent: bfloat16 [16, 128, 32, 2048], P('rep', None, None, 'track'), may hold values from -0.005859375 to 0.005859375
Outputs:
- feature_map: bfloat16 [16, 128, 32, 2048], P('rep', None, None, 'track')
- grad_one: float32 [5, 5, 32, 128], replicated
- grad_two: float32 [3, 3, 128, 128], replicated
The draws below stay inside these ranges and needn't reach their ends.
All inputs are finite; a program needn't handle non-finite values.
Results may differ from the reference program's by a relative error of at most 0.006.
Values may be sent and summed in bfloat16 or wider, within the bound.
No kernel may reach another device: no remote copies, remote signals or barrier semaphores. Data moves between devices by JAX's collectives and lax.ppermute only.
A program may use at most 64 MiB of HBM per device.

```python
import jax
import jax.numpy as jnp
from jax import lax

CIN = 32
FEAT = 128
ROWS = 32
WIDTH = 2048
SAMPLES = 16
CELLS = 1048576


def steps_of(rng, extent, pieces, smallest, high):
    def one(axis_at, blocks):
        draws = jax.random.uniform(jax.random.fold_in(jax.random.fold_in(rng, 6), axis_at), (blocks,), jnp.float32, smallest / len(pieces), high / len(pieces))
        return jnp.repeat(jnp.exp(draws), extent[axis_at] // blocks).reshape((-1,) + (1,) * (len(extent) - axis_at - 1))

    loudness = one(*pieces[0])
    for cut in pieces[1:]:
        loudness = loudness * one(*cut)
    return loudness


def normal_values(key, shape, scale, limit, cuts=(), dtype=jnp.bfloat16):
    factor_of = steps_of(key, shape, cuts, -0.22, 0.18) if cuts else 1.0
    result = jax.random.normal(key, shape, jnp.float32) * scale * factor_of
    return jnp.minimum(jnp.maximum(result, -limit), limit).astype(dtype)


def setup_inputs(seed: int = 0) -> dict:
    keys = jax.random.split(jax.random.key(seed), 5)
    features = normal_values(keys[0], (SAMPLES, CIN, ROWS, WIDTH), 1.0, 6.0, ((0, 16), (3, 16)))
    kernel_one = normal_values(keys[1], (5, 5, CIN, FEAT), (25 * CIN) ** -0.5, 0.21875)
    kernel_two = normal_values(keys[2], (3, 3, FEAT, FEAT), (9 * FEAT) ** -0.5, 0.1875)
    cotangent = normal_values(keys[3], (SAMPLES, FEAT, ROWS, WIDTH), (CELLS ** -0.5), 0.005859375, ((0, 16), (3, 16)))
    return dict(features=features, kernel_one=kernel_one, kernel_two=kernel_two, cotangent=cotangent)


scale_a = 0.7978845608
scale_b = 0.044715

def gelu(values):
    tangent = jnp.tanh(scale_a * (values + scale_b * values * values * values))
    return 0.5 * values * (1.0 + tangent)

def gelu_slope(values):
    tangent = jnp.tanh(scale_a * (values + scale_b * values * values * values))
    return 0.5 * (1.0 + tangent) + 0.5 * values * (1.0 - tangent * tangent) * scale_a * (1.0 + 3.0 * scale_b * values * values)

def convolve(lhs, kernel, dilation):
    return lax.conv_general_dilated(lhs.astype(jnp.float32), kernel.astype(jnp.float32), (1, 1), ((2, 2), (2, 2)), rhs_dilation=(dilation, dilation), dimension_numbers=('NCHW', 'HWIO', 'NCHW'), precision=lax.Precision.HIGHEST)

def reference(features, kernel_one, kernel_two, cotangent):
    first = kernel_one.astype(jnp.float32)
    second = kernel_two.astype(jnp.float32)

    def per_strip(carry, inputs):
        sample, cot_sample = inputs
        sample = sample[None].astype(jnp.float32)
        pre_one = convolve(sample, first, 1)
        hidden = gelu(pre_one).astype(jnp.bfloat16)
        pre_two = convolve(hidden, second, 2)
        output = gelu(pre_two).astype(jnp.bfloat16)
        delta_two = (cot_sample[None].astype(jnp.float32) * gelu_slope(pre_two)).astype(jnp.bfloat16)
        unused, pull_two = jax.vjp(lambda lhs, kernel: convolve(lhs, kernel, 2), hidden.astype(jnp.float32), second)
        back_hidden, grad_two = pull_two(delta_two.astype(jnp.float32))
        delta_one = (back_hidden * gelu_slope(pre_one)).astype(jnp.bfloat16)
        unused_one, pull_one = jax.vjp(lambda kernel: convolve(sample, kernel, 1), first)
        grad_one, = pull_one(delta_one.astype(jnp.float32))
        return ((carry[0] + grad_one, carry[1] + grad_two), output[0])
    init = (jnp.zeros(kernel_one.shape, jnp.float32), jnp.zeros(kernel_two.shape, jnp.float32))
    totals, feature_map = lax.scan(per_strip, init, (features, cotangent))
    return (feature_map, totals[0], totals[1])
```

```python
import jax
import jax.numpy as jnp
from jax import lax
from jax.experimental import pallas as pl
from jax.experimental.pallas import tpu as pltpu
from jax.sharding import Mesh, PartitionSpec as P

scale_a = 0.7978845608
scale_b = 0.044715
BF = jnp.bfloat16
F32 = jnp.float32
ONE = 12
TWO = 8
BACK = 12
SUM_TWO = 16
SUM_ONE = 12


def gelu_and_slope(v):
    v2 = v * v
    t = jnp.tanh(v * (scale_a + (scale_a * scale_b) * v2))
    half = 0.5 * v
    value = half + half * t
    slope = 0.5 + 0.5 * t + half * (1.0 - t * t) * (scale_a + (3.0 * scale_a * scale_b) * v2)
    return value, slope


def shifted(v, shift):
    rows = v.shape[1]
    h = lax.broadcasted_iota(jnp.int32, v.shape, 1)
    rolled = pltpu.roll(v, (-shift) % rows, 1)
    keep = (h < rows - shift) if shift > 0 else (h >= -shift)
    return jnp.where(keep, rolled, 0.0)


def flat(v):
    return v.reshape(v.shape[0] * v.shape[1], v.shape[2])


def over_rows(a, b):
    return lax.dot_general(a, b, (((0,), (0,)), ((), ())), preferred_element_type=F32)


def block_kernel(
    place, low, middle, high, k1, k2, k2t, cot, fmap, keep, send,
    xe, taps, bottom, tail, hid, slope, delta, dlast, acc2, acc1, total,
):
    xe[0:4] = low[...]
    xe[4:132] = middle[...]
    xe[132:136] = high[...]

    def row_taps(n, carry):
        at = pl.ds(n * 8, 8)
        v = xe[at].astype(F32)
        lane = lax.broadcasted_iota(jnp.int32, v.shape, 2)
        taps[at] = jnp.where(
            lane < 64,
            jnp.where(lane < 32, shifted(v, -2), shifted(v, -1)),
            jnp.where(lane < 96, v, shifted(v, 1)),
        ).astype(BF)
        bottom[at] = shifted(v, 2).astype(BF)
        return carry

    lax.fori_loop(0, 17, row_taps, 0)

    def last_row_taps(n, carry):
        at = n * 12
        lane = lax.broadcasted_iota(jnp.int32, (12, 32, 128), 2)
        s = [bottom[pl.ds(at + j, 12)] for j in range(4)]
        tail[pl.ds(at, 12)] = jnp.where(
            lane < 64, jnp.where(lane < 32, s[0], s[1]), jnp.where(lane < 96, s[2], s[3])
        )
        return carry

    lax.fori_loop(0, 11, last_row_taps, 0)

    def windows_one(at, n):
        parts = [taps[pl.ds(at + j, n)] for j in range(5)]
        parts += [tail[pl.ds(at, n)], bottom[pl.ds(at + 4, n)]]
        return jnp.concatenate([flat(x) for x in parts], axis=1)

    def windows_two(at, n):
        parts = [hid[i, pl.ds(at + 2 * j, n)] for i in range(3) for j in range(3)]
        return jnp.concatenate([flat(x) for x in parts], axis=1)

    def first(n, carry):
        at = n * ONE
        pre = jnp.dot(windows_one(at, ONE), k1[...], preferred_element_type=F32)
        h, s = gelu_and_slope(pre.reshape(ONE, 32, 128))
        slope[pl.ds(at, ONE)] = s
        hid[0, pl.ds(at, ONE)] = shifted(h, -2).astype(BF)
        hid[1, pl.ds(at, ONE)] = h.astype(BF)
        hid[2, pl.ds(at, ONE)] = shifted(h, 2).astype(BF)
        return carry

    lax.fori_loop(0, 132 // ONE, first, 0)

    @pl.when(place[0] == 0)
    def _():
        hid[:, 0:2] = jnp.zeros((3, 2, 32, 128), BF)
        slope[0:2] = jnp.zeros((2, 32, 128), F32)

    @pl.when(place[1] == 0)
    def _():
        hid[:, 130:132] = jnp.zeros((3, 2, 32, 128), BF)
        slope[130:132] = jnp.zeros((2, 32, 128), F32)

    delta[:, 0:4] = jnp.zeros((3, 4, 32, 128), BF)
    delta[:, 132:136] = jnp.zeros((3, 4, 32, 128), BF)

    def second(n, carry):
        at = n * TWO
        pre = jnp.dot(windows_two(at, TWO), k2[...], preferred_element_type=F32)
        f, s = gelu_and_slope(pre.reshape(TWO, 32, 128))
        fmap[pl.ds(at, TWO)] = f.astype(BF)
        d = cot[pl.ds(at, TWO)].astype(F32) * s
        delta[0, pl.ds(at + 4, TWO)] = shifted(d, 2).astype(BF)
        delta[1, pl.ds(at + 4, TWO)] = d.astype(BF)
        delta[2, pl.ds(at + 4, TWO)] = shifted(d, -2).astype(BF)
        return carry

    lax.fori_loop(0, 128 // TWO, second, 0)

    acc2[...] = jnp.zeros(acc2.shape, F32)
    acc1[...] = jnp.zeros(acc1.shape, F32)

    def sum_two(n, carry):
        at = n * SUM_TWO
        d = flat(delta[1, pl.ds(at + 4, SUM_TWO)])
        acc2[...] += over_rows(d, windows_two(at, SUM_TWO))
        return carry

    lax.fori_loop(0, 128 // SUM_TWO, sum_two, 0)

    def back(n, carry):
        at = n * BACK
        parts = [delta[i, pl.ds(at + 4 - 2 * j, BACK)] for i in range(3) for j in range(3)]
        lhs = jnp.concatenate([flat(x) for x in parts], axis=1)
        b = jnp.dot(lhs, k2t[...], preferred_element_type=F32)
        dlast[pl.ds(at, BACK)] = (b.reshape(BACK, 32, 128) * slope[pl.ds(at, BACK)]).astype(BF)
        return carry

    lax.fori_loop(0, 132 // BACK, back, 0)

    def sum_one(n, carry):
        at = n * SUM_ONE
        d = flat(dlast[pl.ds(at, SUM_ONE)])
        acc1[...] += over_rows(d, windows_one(at, SUM_ONE))
        return carry

    lax.fori_loop(0, 132 // SUM_ONE, sum_one, 0)

    total[0:1152] = acc2[...].T
    a1 = acc1[...].T
    for i in range(5):
        for j in range(5):
            row = j * 128 + i * 32 if i < 4 else 640 + j * 32
            to = 1152 + (i * 5 + j) * 32
            total[to : to + 32] = a1[row : row + 32]
    total[1952:2048] = jnp.zeros((96, 128), F32)
    mine = pl.multiple_of(place[2] * 1024, 1024)
    other = pl.multiple_of((1 - place[2]) * 1024, 1024)
    keep[...] = total[pl.ds(mine, 1024)]
    send[...] = total[pl.ds(other, 1024)].astype(BF)


def block(place, low, middle, high, k1, k2, k2t, cot):
    vmem = pl.BlockSpec(memory_space=pltpu.VMEM)
    return pl.pallas_call(
        block_kernel,
        out_shape=(
            jax.ShapeDtypeStruct((128, 32, 128), BF),
            jax.ShapeDtypeStruct((1024, 128), F32),
            jax.ShapeDtypeStruct((1024, 128), BF),
        ),
        in_specs=[pl.BlockSpec(memory_space=pltpu.SMEM)] + [vmem] * 7,
        out_specs=(vmem, vmem, vmem),
        scratch_shapes=[
            pltpu.VMEM((136, 32, 128), BF),
            pltpu.VMEM((136, 32, 128), BF),
            pltpu.VMEM((136, 32, 128), BF),
            pltpu.VMEM((132, 32, 128), BF),
            pltpu.VMEM((3, 132, 32, 128), BF),
            pltpu.VMEM((132, 32, 128), F32),
            pltpu.VMEM((3, 136, 32, 128), BF),
            pltpu.VMEM((132, 32, 128), BF),
            pltpu.VMEM((128, 1152), F32),
            pltpu.VMEM((128, 896), F32),
            pltpu.VMEM((2048, 128), F32),
        ],
        compiler_params=pltpu.CompilerParams(vmem_limit_bytes=50 * 1024 * 1024),
        cost_estimate=pl.CostEstimate(
            flops=5_500_000_000, bytes_accessed=5_000_000, transcendentals=1_100_000
        ),
    )(place, low, middle, high, k1, k2, k2t, cot)


def kernel_rows(kernel_one, kernel_two):
    first = kernel_one[:4].transpose(1, 0, 2, 3).reshape(640, 128)
    last = kernel_one[4].reshape(160, 128)
    k1 = jnp.concatenate([first, last, jnp.zeros((96, 128), BF)], 0)
    k2 = kernel_two.reshape(1152, 128)
    k2t = kernel_two.transpose(0, 1, 3, 2).reshape(1152, 128)
    return k1, k2, k2t


def columns_first(block_of):
    return jnp.transpose(block_of[0], (2, 1, 0))


def fourfold(v):
    return jnp.tile(v, (1, 1, 4))


TRACK = ("y", "zh")
REP = ("x", "zl", "core")
CHIPS = ("y", "zh", "x", "zl")


def on_device(features, kernel_one, kernel_two, cotangent):
    at = lax.axis_index(TRACK)
    core = lax.axis_index("core")
    up = [(i, i + 1) for i in range(15)]
    down = [(i + 1, i) for i in range(15)]
    low = lax.ppermute(fourfold(columns_first(features[..., 124:])), TRACK, up)
    high = lax.ppermute(fourfold(columns_first(features[..., :4])), TRACK, down)
    middle = fourfold(columns_first(features))
    k1, k2, k2t = kernel_rows(kernel_one, kernel_two)
    place = jnp.stack([(at > 0).astype(jnp.int32), (at < 15).astype(jnp.int32), core])
    fmap, keep, send = block(place, low, middle, high, k1, k2, k2t, columns_first(cotangent))
    feature_map = jnp.transpose(fmap, (2, 1, 0))[None]
    swap = [(0, 1), (1, 0)]
    chip_sum = (keep + lax.ppermute(send, "core", swap).astype(F32)).astype(BF)
    parts = lax.all_to_all(chip_sum.reshape(128, 8, 128), CHIPS, 0, 0, tiled=True)
    mine = jnp.sum(parts.astype(F32), axis=0).astype(BF)
    spread = jnp.broadcast_to(mine[None], (128, 8, 128))
    half = lax.all_to_all(spread, CHIPS, 0, 0, tiled=True).reshape(1024, 128)
    rest = lax.ppermute(half, "core", swap)
    rows = jnp.concatenate(
        [jnp.where(core == 0, half, rest), jnp.where(core == 0, rest, half)], axis=0
    ).astype(F32)
    grad_two = rows[:1152].reshape(3, 3, 128, 128)
    grad_one = rows[1152:1952].reshape(5, 5, 32, 128)
    return (feature_map, grad_one, grad_two)


def solution(mesh):
    fine = Mesh(mesh.devices.reshape(4, 4, 4, 2, 2), TRACK + REP)
    placed = (P(REP, None, None, TRACK), P(), P(), P(REP, None, None, TRACK))
    return jax.shard_map(
        on_device,
        mesh=fine,
        in_specs=placed,
        out_specs=(P(REP, None, None, TRACK), P(), P()),
        check_vma=False,
    )
```

```python
import jax
import jax.numpy as jnp
from jax import lax
from jax.experimental import pallas as pl
from jax.experimental.pallas import tpu as pltpu
from jax.sharding import Mesh, PartitionSpec as P

scale_a = 0.7978845608
scale_b = 0.044715
BF = jnp.bfloat16
F32 = jnp.float32
ONE = 22
TWO = 8
BACK = 11


def gelu_and_slope(v):
    c = (scale_a * scale_b) * (v * v)
    t = jnp.tanh(v * (scale_a + c))
    p = 0.5 + 0.5 * t
    value = v * p
    slope = p + value * (scale_a + 3.0 * c) * (1.0 - t)
    return value, slope


def shifted(v, shift):
    rows = v.shape[1]
    h = lax.broadcasted_iota(jnp.int32, v.shape, 1)
    rolled = pltpu.roll(v, (-shift) % rows, 1)
    keep = (h < rows - shift) if shift > 0 else (h >= -shift)
    return jnp.where(keep, rolled, jnp.zeros_like(rolled))


def row_copies(v):
    v = v.astype(BF)
    z = jnp.zeros((v.shape[0], 2, v.shape[2]), BF)
    return jnp.concatenate([z, v[:, :-2]], axis=1), v, jnp.concatenate([v[:, 2:], z], axis=1)


def over_rows(a, b):
    return lax.dot_general(a, b, (((0,), (0,)), ((), ())), preferred_element_type=F32)


def block_kernel(
    place, low, middle, high, k1, k2, cot, fmap, keep, send,
    xe, taps, bottom, tail, hid, slope, delta, pairs2, pairs1, w1, w2, wb, acc2, acc1, total,
):
    zero = jnp.zeros((32, 128), BF)
    for k in range(6):
        for r in range(2):
            j = k - r
            for i in range(5):
                row = k * 128 + i * 32 if i < 4 else 768 + k * 32
                w1[row : row + 32, r * 128 : r * 128 + 128] = k1[i, j] if 0 <= j < 5 else zero
    w1[960:1024] = jnp.zeros((64, 256), BF)
    square = jnp.zeros((128, 128), BF)
    for i in range(3):
        for s in range(2):
            lanes = slice(s * 128, s * 128 + 128)
            for k in range(4):
                rows = slice((i * 4 + k) * 128, (i * 4 + k) * 128 + 128)
                j = k - s
                w2[rows, lanes] = k2[i, j] if 0 <= j < 3 else square
                j = s + 2 - k
                wb[rows, lanes] = k2[i, j].T if 0 <= j < 3 else square

    xe[0:4] = low[...]
    xe[4:132] = middle[...]
    xe[132:136] = high[...]
    bottom[136:140] = jnp.zeros((4, 32, 128), BF)

    def row_taps(n, carry):
        at = pl.ds(n * 34, 34)
        v = xe[at].astype(F32)
        lane = lax.broadcasted_iota(jnp.int32, v.shape, 2)
        taps[at] = jnp.where(
            lane < 64,
            jnp.where(lane < 32, shifted(v, -2), shifted(v, -1)),
            jnp.where(lane < 96, v, shifted(v, 1)),
        ).astype(BF)
        bottom[at] = shifted(v, 2).astype(BF)
        return carry

    lax.fori_loop(0, 4, row_taps, 0)
    lane = lax.broadcasted_iota(jnp.int32, (32, 128), 1)
    for v in range(68):
        s = [bottom[2 * v + k] for k in range(4)]
        tail[v] = jnp.where(
            lane < 64, jnp.where(lane < 32, s[0], s[1]), jnp.where(lane < 96, s[2], s[3])
        )

    def windows_one(v, n):
        parts = [jnp.concatenate([taps[2 * (v + t) + k] for t in range(n)], 0) for k in range(6)]
        parts += [tail[pl.ds(v + d, n)].reshape(n * 32, 128) for d in (0, 2)]
        return jnp.concatenate(parts, axis=1)

    def windows_two(ref, q, n):
        parts = [
            jnp.concatenate([ref[i, 2 * (q + t) + k] for t in range(n)], 0)
            for i in range(3)
            for k in range(4)
        ]
        return jnp.concatenate(parts, axis=1)

    def first(m, carry):
        v = m * ONE
        pre = jnp.dot(windows_one(v, ONE), w1[...], preferred_element_type=F32)
        for r in range(2):
            h, s = gelu_and_slope(pre[:, r * 128 : r * 128 + 128].reshape(ONE, 32, 128))
            at = (pl.ds(v, ONE), slice(r * 32, r * 32 + 32))
            slope[at] = s
            for i, copy in enumerate(row_copies(h)):
                hid[(i,) + at] = copy
        return carry

    lax.fori_loop(0, 66 // ONE, first, 0)

    @pl.when(place[0] == 0)
    def _():
        hid[:, 0] = jnp.zeros((3, 64, 128), BF)
        slope[0] = jnp.zeros((64, 128), F32)

    @pl.when(place[1] == 0)
    def _():
        hid[:, 65] = jnp.zeros((3, 64, 128), BF)
        slope[65] = jnp.zeros((64, 128), F32)

    delta[:, 0:2] = jnp.zeros((3, 2, 64, 128), BF)
    delta[:, 66:68] = jnp.zeros((3, 2, 64, 128), BF)

    def second(m, carry):
        q = m * TWO
        pre = jnp.dot(windows_two(hid, q, TWO), w2[...], preferred_element_type=F32)
        for s in range(2):
            f, sl = gelu_and_slope(pre[:, s * 128 : s * 128 + 128].reshape(TWO, 64, 128))
            fmap[pl.ds(q, TWO), s] = f.astype(BF)
            d = cot[pl.ds(q, TWO), s].astype(F32) * sl
            pairs2[pl.ds(q, TWO), :, s * 128 : s * 128 + 128] = d.astype(BF)
            for i, copy in enumerate(reversed(row_copies(d.reshape(TWO * 2, 32, 128)))):
                copy = copy.reshape(TWO, 64, 128)
                for t in range(TWO):
                    delta[i, 2 * (q + t) + 2 + s] = copy[t]
        return carry

    lax.fori_loop(0, 32 // TWO, second, 0)
    acc2[...] = over_rows(pairs2[...].reshape(2048, 256), windows_two(hid, 0, 32))

    def back(m, carry):
        q = m * BACK
        both = jnp.dot(windows_two(delta, q, BACK), wb[...], preferred_element_type=F32)
        for s in range(2):
            b = both[:, s * 128 : s * 128 + 128].reshape(BACK, 64, 128)
            for t in range(BACK):
                v = 2 * (q + t) + s
                d = (b[t] * slope[v]).astype(BF)
                pairs1[v, :, 0:128] = d[0:32]
                pairs1[v, :, 128:256] = d[32:64]
        return carry

    lax.fori_loop(0, 33 // BACK, back, 0)
    acc1[...] = over_rows(pairs1[...].reshape(2112, 256), windows_one(0, 66))

    for i in range(3):
        for j in range(3):
            at = (i * 4 + j) * 128
            to = (i * 3 + j) * 128
            both = acc2[0:128, at : at + 128] + acc2[128:256, at + 128 : at + 256]
            total[to : to + 128] = both.T
    for j in range(5):
        at = j * 128
        both = (acc1[0:128, at : at + 128] + acc1[128:256, at + 128 : at + 256]).T
        for i in range(4):
            to = 1152 + (i * 5 + j) * 32
            total[to : to + 32] = both[i * 32 : i * 32 + 32]
    even = acc1[0:128, 768:1024].T
    odd = acc1[128:256, 768:1024].T
    total[1792:1952] = even[0:160] + odd[32:192]
    total[1952:2048] = jnp.zeros((96, 128), F32)
    mine = pl.multiple_of(place[2] * 1024, 1024)
    other = pl.multiple_of((1 - place[2]) * 1024, 1024)
    keep[...] = total[pl.ds(mine, 1024)]
    send[...] = total[pl.ds(other, 1024)].astype(BF)


def block(place, low, middle, high, k1, k2, cot):
    vmem = pl.BlockSpec(memory_space=pltpu.VMEM)
    return pl.pallas_call(
        block_kernel,
        out_shape=(
            jax.ShapeDtypeStruct((32, 2, 64, 128), BF),
            jax.ShapeDtypeStruct((1024, 128), F32),
            jax.ShapeDtypeStruct((1024, 128), BF),
        ),
        in_specs=[pl.BlockSpec(memory_space=pltpu.SMEM)] + [vmem] * 6,
        out_specs=(vmem, vmem, vmem),
        scratch_shapes=[
            pltpu.VMEM((136, 32, 128), BF),
            pltpu.VMEM((136, 32, 128), BF),
            pltpu.VMEM((140, 32, 128), BF),
            pltpu.VMEM((68, 32, 128), BF),
            pltpu.VMEM((3, 66, 64, 128), BF),
            pltpu.VMEM((66, 64, 128), F32),
            pltpu.VMEM((3, 68, 64, 128), BF),
            pltpu.VMEM((32, 64, 256), BF),
            pltpu.VMEM((66, 32, 256), BF),
            pltpu.VMEM((1024, 256), BF),
            pltpu.VMEM((1536, 256), BF),
            pltpu.VMEM((1536, 256), BF),
            pltpu.VMEM((256, 1536), F32),
            pltpu.VMEM((256, 1024), F32),
            pltpu.VMEM((2048, 128), F32),
        ],
        compiler_params=pltpu.CompilerParams(vmem_limit_bytes=45 * 1024 * 1024),
        cost_estimate=pl.CostEstimate(
            flops=5_500_000_000, bytes_accessed=5_000_000, transcendentals=1_100_000
        ),
    )(place, low, middle, high, k1, k2, cot.reshape(32, 2, 64, 128))


def columns_first(block_of):
    return jnp.transpose(block_of[0], (2, 1, 0))


def fourfold(v):
    return jnp.tile(v, (1, 1, 4))


TRACK = ("y", "zh")
REP = ("x", "zl", "core")


def exchange(pieces, axes):
    return lax.all_to_all(pieces, axes, 0, 0, tiled=True)


def gathered(piece, axes, count):
    return exchange(jnp.broadcast_to(piece[None], (count,) + piece.shape), axes)


def summed(pieces):
    return jnp.sum(pieces.astype(F32), axis=0).astype(BF)


def on_device(features, kernel_one, kernel_two, cotangent):
    at = lax.axis_index(TRACK)
    core = lax.axis_index("core")
    up = [(i, i + 1) for i in range(15)]
    down = [(i + 1, i) for i in range(15)]
    middle = fourfold(columns_first(features))
    low = lax.ppermute(middle[124:], TRACK, up)
    high = lax.ppermute(middle[:4], TRACK, down)
    place = jnp.stack([(at > 0).astype(jnp.int32), (at < 15).astype(jnp.int32), core])
    fmap, keep, send = block(
        place, low, middle, high, kernel_one, kernel_two, columns_first(cotangent)
    )
    feature_map = jnp.transpose(fmap.reshape(128, 32, 128), (2, 1, 0))[None]
    swap = [(0, 1), (1, 0)]
    chip_sum = (keep + lax.ppermute(send, "core", swap).astype(F32)).astype(BF)
    layer_sum = summed(exchange(chip_sum.reshape(16, 64, 128), ("x", "y")))
    full_sum = summed(gathered(layer_sum, ("zh", "zl"), 8))
    half = gathered(full_sum, ("x", "y"), 16).reshape(1024, 128)
    rest = lax.ppermute(half, "core", swap)
    rows = jnp.concatenate(
        [jnp.where(core == 0, half, rest), jnp.where(core == 0, rest, half)], axis=0
    ).astype(F32)
    grad_two = rows[:1152].reshape(3, 3, 128, 128)
    grad_one = rows[1152:1952].reshape(5, 5, 32, 128)
    return (feature_map, grad_one, grad_two)


def solution(mesh):
    fine = Mesh(mesh.devices.reshape(4, 4, 4, 2, 2), TRACK + REP)
    placed = (P(REP, None, None, TRACK), P(), P(), P(REP, None, None, TRACK))
    return jax.shard_map(
        on_device,
        mesh=fine,
        in_specs=placed,
        out_specs=(P(REP, None, None, TRACK), P(), P()),
        check_vma=False,
    )
```

```python
import jax
import jax.numpy as jnp
from jax import lax
from jax.experimental import pallas as pl
from jax.experimental.pallas import tpu as pltpu
from jax.sharding import Mesh, PartitionSpec as P

scale_a = 0.7978845608
scale_b = 0.044715
BF = jnp.bfloat16
F32 = jnp.float32
ONE = 6
TWO = 2
BACK = 3


def gelu_and_slope(v):
    c = (scale_a * scale_b) * (v * v)
    t = jnp.tanh(v * (scale_a + c))
    p = 0.5 + 0.5 * t
    value = v * p
    slope = p + value * (scale_a + 3.0 * c) * (1.0 - t)
    return value, slope


def shifted(v, shift):
    rows = v.shape[1]
    h = lax.broadcasted_iota(jnp.int32, v.shape, 1)
    rolled = pltpu.roll(v, (-shift) % rows, 1)
    keep = (h < rows - shift) if shift > 0 else (h >= -shift)
    return jnp.where(keep, rolled, jnp.zeros_like(rolled))


def row_copies(v):
    v = v.astype(BF)
    z = jnp.zeros((v.shape[0], 2, v.shape[2]), BF)
    return jnp.concatenate([z, v[:, :-2]], axis=1), v, jnp.concatenate([v[:, 2:], z], axis=1)


def over_rows(a, b):
    return lax.dot_general(a, b, (((0,), (0,)), ((), ())), preferred_element_type=F32)


def block_kernel(
    place, low, middle, high, k1, k2, cot, fmap, keep, send,
    xe, taps, bottom, tail, hid, slope, delta, pairs2, pairs1, w1, w2, wb, acc2, acc1, total,
):
    zero = jnp.zeros((32, 128), BF)
    for k in range(6):
        for r in range(2):
            j = k - r
            for i in range(5):
                row = k * 128 + i * 32 if i < 4 else 768 + k * 32
                w1[row : row + 32, r * 128 : r * 128 + 128] = k1[i, j] if 0 <= j < 5 else zero
    w1[960:1024] = jnp.zeros((64, 256), BF)
    square = jnp.zeros((128, 128), BF)
    for i in range(3):
        for s in range(2):
            lanes = slice(s * 128, s * 128 + 128)
            for k in range(4):
                rows = slice((i * 4 + k) * 128, (i * 4 + k) * 128 + 128)
                j = k - s
                w2[rows, lanes] = k2[i, j] if 0 <= j < 3 else square
                j = s + 2 - k
                wb[rows, lanes] = k2[i, j].T if 0 <= j < 3 else square

    xe[0:4] = low[...]
    xe[4:132] = middle[...]
    xe[132:136] = high[...]
    bottom[136:140] = jnp.zeros((4, 32, 128), BF)

    def row_taps(n, carry):
        at = pl.ds(n * 34, 34)
        v = xe[at].astype(F32)
        lane = lax.broadcasted_iota(jnp.int32, v.shape, 2)
        taps[at] = jnp.where(
            lane < 64,
            jnp.where(lane < 32, shifted(v, -2), shifted(v, -1)),
            jnp.where(lane < 96, v, shifted(v, 1)),
        ).astype(BF)
        bottom[at] = shifted(v, 2).astype(BF)
        return carry

    lax.fori_loop(0, 4, row_taps, 0)
    lane = lax.broadcasted_iota(jnp.int32, (32, 128), 1)
    for v in range(68):
        s = [bottom[2 * v + k] for k in range(4)]
        tail[v] = jnp.where(
            lane < 64, jnp.where(lane < 32, s[0], s[1]), jnp.where(lane < 96, s[2], s[3])
        )

    def windows_one(v, n):
        parts = [jnp.concatenate([taps[2 * (v + t) + k] for t in range(n)], 0) for k in range(6)]
        parts += [tail[pl.ds(v + d, n)].reshape(n * 32, 128) for d in (0, 2)]
        return jnp.concatenate(parts, axis=1)

    def windows_two(ref, q, n):
        parts = [
            jnp.concatenate([ref[i, 2 * (q + t) + k] for t in range(n)], 0)
            for i in range(3)
            for k in range(4)
        ]
        return jnp.concatenate(parts, axis=1)

    def first(m, carry):
        v = m * ONE
        pre = jnp.dot(windows_one(v, ONE), w1[...], preferred_element_type=F32)
        for r in range(2):
            h, s = gelu_and_slope(pre[:, r * 128 : r * 128 + 128].reshape(ONE, 32, 128))
            at = (pl.ds(v, ONE), slice(r * 32, r * 32 + 32))
            slope[at] = s
            for i, copy in enumerate(row_copies(h)):
                hid[(i,) + at] = copy
        return carry

    lax.fori_loop(0, 66 // ONE, first, 0, unroll=True)

    @pl.when(place[0] == 0)
    def _():
        hid[:, 0] = jnp.zeros((3, 64, 128), BF)
        slope[0] = jnp.zeros((64, 128), F32)

    @pl.when(place[1] == 0)
    def _():
        hid[:, 65] = jnp.zeros((3, 64, 128), BF)
        slope[65] = jnp.zeros((64, 128), F32)

    delta[:, 0:2] = jnp.zeros((3, 2, 64, 128), BF)
    delta[:, 66:68] = jnp.zeros((3, 2, 64, 128), BF)

    def second(m, carry):
        q = m * TWO
        pre = jnp.dot(windows_two(hid, q, TWO), w2[...], preferred_element_type=F32)
        for s in range(2):
            f, sl = gelu_and_slope(pre[:, s * 128 : s * 128 + 128].reshape(TWO, 64, 128))
            fmap[pl.ds(q, TWO), s] = f.astype(BF)
            d = cot[pl.ds(q, TWO), s].astype(F32) * sl
            pairs2[pl.ds(q, TWO), :, s * 128 : s * 128 + 128] = d.astype(BF)
            for i, copy in enumerate(reversed(row_copies(d.reshape(TWO * 2, 32, 128)))):
                copy = copy.reshape(TWO, 64, 128)
                for t in range(TWO):
                    delta[i, 2 * (q + t) + 2 + s] = copy[t]
        return carry

    lax.fori_loop(0, 32 // TWO, second, 0, unroll=True)
    acc2[...] = over_rows(pairs2[...].reshape(2048, 256), windows_two(hid, 0, 32))

    def back(m, carry):
        q = m * BACK
        both = jnp.dot(windows_two(delta, q, BACK), wb[...], preferred_element_type=F32)
        for s in range(2):
            b = both[:, s * 128 : s * 128 + 128].reshape(BACK, 64, 128)
            for t in range(BACK):
                v = 2 * (q + t) + s
                d = (b[t] * slope[v]).astype(BF)
                pairs1[v, :, 0:128] = d[0:32]
                pairs1[v, :, 128:256] = d[32:64]
        return carry

    lax.fori_loop(0, 33 // BACK, back, 0, unroll=True)
    acc1[...] = over_rows(pairs1[...].reshape(2112, 256), windows_one(0, 66))

    for i in range(3):
        for j in range(3):
            at = (i * 4 + j) * 128
            to = (i * 3 + j) * 128
            both = acc2[0:128, at : at + 128] + acc2[128:256, at + 128 : at + 256]
            total[to : to + 128] = both.T
    for j in range(5):
        at = j * 128
        both = (acc1[0:128, at : at + 128] + acc1[128:256, at + 128 : at + 256]).T
        for i in range(4):
            to = 1152 + (i * 5 + j) * 32
            total[to : to + 32] = both[i * 32 : i * 32 + 32]
    even = acc1[0:128, 768:1024].T
    odd = acc1[128:256, 768:1024].T
    total[1792:1952] = even[0:160] + odd[32:192]
    total[1952:2048] = jnp.zeros((96, 128), F32)
    mine = pl.multiple_of(place[2] * 1024, 1024)
    other = pl.multiple_of((1 - place[2]) * 1024, 1024)
    keep[...] = total[pl.ds(mine, 1024)]
    send[...] = total[pl.ds(other, 1024)].astype(BF)


def block(place, low, middle, high, k1, k2, cot):
    vmem = pl.BlockSpec(memory_space=pltpu.VMEM)
    return pl.pallas_call(
        block_kernel,
        out_shape=(
            jax.ShapeDtypeStruct((32, 2, 64, 128), BF),
            jax.ShapeDtypeStruct((1024, 128), F32),
            jax.ShapeDtypeStruct((1024, 128), BF),
        ),
        in_specs=[pl.BlockSpec(memory_space=pltpu.SMEM)] + [vmem] * 6,
        out_specs=(vmem, vmem, vmem),
        scratch_shapes=[
            pltpu.VMEM((136, 32, 128), BF),
            pltpu.VMEM((136, 32, 128), BF),
            pltpu.VMEM((140, 32, 128), BF),
            pltpu.VMEM((68, 32, 128), BF),
            pltpu.VMEM((3, 66, 64, 128), BF),
            pltpu.VMEM((66, 64, 128), F32),
            pltpu.VMEM((3, 68, 64, 128), BF),
            pltpu.VMEM((32, 64, 256), BF),
            pltpu.VMEM((66, 32, 256), BF),
            pltpu.VMEM((1024, 256), BF),
            pltpu.VMEM((1536, 256), BF),
            pltpu.VMEM((1536, 256), BF),
            pltpu.VMEM((256, 1536), F32),
            pltpu.VMEM((256, 1024), F32),
            pltpu.VMEM((2048, 128), F32),
        ],
        compiler_params=pltpu.CompilerParams(vmem_limit_bytes=45 * 1024 * 1024),
        cost_estimate=pl.CostEstimate(
            flops=5_500_000_000, bytes_accessed=5_000_000, transcendentals=1_100_000
        ),
    )(place, low, middle, high, k1, k2, cot.reshape(32, 2, 64, 128))


def columns_first(block_of):
    return jnp.transpose(block_of[0], (2, 1, 0))


def fourfold(v):
    return jnp.tile(v, (1, 1, 4))


TRACK = ("y", "zh")
REP = ("x", "zl", "core")


def exchange(pieces, axes):
    return lax.all_to_all(pieces, axes, 0, 0, tiled=True)


def gathered(piece, axes, count):
    return exchange(jnp.broadcast_to(piece[None], (count,) + piece.shape), axes)


def summed(pieces):
    return jnp.sum(pieces.astype(F32), axis=0).astype(BF)


def on_device(features, kernel_one, kernel_two, cotangent):
    at = lax.axis_index(TRACK)
    core = lax.axis_index("core")
    up = [(i, i + 1) for i in range(15)]
    down = [(i + 1, i) for i in range(15)]
    middle = lax.optimization_barrier(fourfold(columns_first(features)))
    low = lax.ppermute(middle[124:], TRACK, up)
    high = lax.ppermute(middle[:4], TRACK, down)
    place = jnp.stack([(at > 0).astype(jnp.int32), (at < 15).astype(jnp.int32), core])
    fmap, keep, send = block(
        place, low, middle, high, kernel_one, kernel_two, columns_first(cotangent)
    )
    feature_map = jnp.transpose(fmap.reshape(128, 32, 128), (2, 1, 0))[None]
    swap = [(0, 1), (1, 0)]
    chip_sum = (keep + lax.ppermute(send, "core", swap).astype(F32)).astype(BF)
    layer_sum = summed(exchange(chip_sum.reshape(16, 64, 128), ("x", "y")))
    full_sum = summed(gathered(layer_sum, ("zh", "zl"), 8))
    half = gathered(full_sum, ("x", "y"), 16).reshape(1024, 128)
    rest = lax.ppermute(half, "core", swap)
    rows = jnp.concatenate(
        [jnp.where(core == 0, half, rest), jnp.where(core == 0, rest, half)], axis=0
    ).astype(F32)
    grad_two = rows[:1152].reshape(3, 3, 128, 128)
    grad_one = rows[1152:1952].reshape(5, 5, 32, 128)
    return (feature_map, grad_one, grad_two)


def solution(mesh):
    fine = Mesh(mesh.devices.reshape(4, 4, 4, 2, 2), TRACK + REP)
    placed = (P(REP, None, None, TRACK), P(), P(), P(REP, None, None, TRACK))
    return jax.shard_map(
        on_device,
        mesh=fine,
        in_specs=placed,
        out_specs=(P(REP, None, None, TRACK), P(), P()),
        check_vma=False,
    )
```

```python
import jax
import jax.numpy as jnp
from jax import lax
from jax.experimental import pallas as pl
from jax.experimental.pallas import tpu as pltpu
from jax.sharding import Mesh, PartitionSpec as P

scale_a = 0.7978845608
scale_b = 0.044715
BF = jnp.bfloat16
F32 = jnp.float32
ONE = 6
TWO = 2
BACK = 3


def gelu_and_slope(v):
    c = (scale_a * scale_b) * (v * v)
    t = jnp.tanh(v * (scale_a + c))
    p = 0.5 + 0.5 * t
    value = v * p
    slope = p + value * (scale_a + 3.0 * c) * (1.0 - t)
    return value, slope


def shifted(v, shift):
    rows = v.shape[1]
    h = lax.broadcasted_iota(jnp.int32, v.shape, 1)
    rolled = pltpu.roll(v, (-shift) % rows, 1)
    keep = (h < rows - shift) if shift > 0 else (h >= -shift)
    return jnp.where(keep, rolled, jnp.zeros_like(rolled))


def row_copies(v):
    v = v.astype(BF)
    z = jnp.zeros((v.shape[0], 2, v.shape[2]), BF)
    return jnp.concatenate([z, v[:, :-2]], axis=1), v, jnp.concatenate([v[:, 2:], z], axis=1)


def over_rows(a, b):
    return lax.dot_general(a, b, (((0,), (0,)), ((), ())), preferred_element_type=F32)


def weights_kernel(k1, k2, w1, w2, wb):
    zero = jnp.zeros((32, 128), BF)
    for k in range(6):
        for r in range(2):
            j = k - r
            for i in range(5):
                row = k * 128 + i * 32 if i < 4 else 768 + k * 32
                w1[row : row + 32, r * 128 : r * 128 + 128] = k1[i, j] if 0 <= j < 5 else zero
    w1[960:1024] = jnp.zeros((64, 256), BF)
    square = jnp.zeros((128, 128), BF)
    for i in range(3):
        for s in range(2):
            lanes = slice(s * 128, s * 128 + 128)
            for k in range(4):
                rows = slice((i * 4 + k) * 128, (i * 4 + k) * 128 + 128)
                j = k - s
                w2[rows, lanes] = k2[i, j] if 0 <= j < 3 else square
                j = s + 2 - k
                wb[rows, lanes] = k2[i, j].T if 0 <= j < 3 else square


def weights(k1, k2):
    vmem = pl.BlockSpec(memory_space=pltpu.VMEM)
    return pl.pallas_call(
        weights_kernel,
        out_shape=(
            jax.ShapeDtypeStruct((1024, 256), BF),
            jax.ShapeDtypeStruct((1536, 256), BF),
            jax.ShapeDtypeStruct((1536, 256), BF),
        ),
        in_specs=[vmem] * 2,
        out_specs=(vmem,) * 3,
        compiler_params=pltpu.CompilerParams(vmem_limit_bytes=8 * 1024 * 1024),
        cost_estimate=pl.CostEstimate(flops=0, bytes_accessed=2_500_000, transcendentals=0),
    )(k1, k2)


def block_kernel(
    place, low, middle, high, w1, w2, wb, cot, fmap, keep, send,
    taps, bottom, tail, hid, slope, delta, pairs2, pairs1, acc2, acc1, total,
):
    bottom[136:140] = jnp.zeros((4, 32, 128), BF)
    lane = lax.broadcasted_iota(jnp.int32, (4, 32, 128), 2)
    for n in range(34):
        at = slice(n * 4, n * 4 + 4)
        x = low[...] if n == 0 else high[...] if n == 33 else middle[n * 4 - 4 : n * 4]
        v = x.astype(F32)
        taps[at] = jnp.where(
            lane < 64,
            jnp.where(lane < 32, shifted(v, -2), shifted(v, -1)),
            jnp.where(lane < 96, v, shifted(v, 1)),
        ).astype(BF)
        bottom[at] = row_copies(x)[2]
    lane = lax.broadcasted_iota(jnp.int32, (32, 128), 1)
    for v in range(68):
        s = [bottom[2 * v + k] for k in range(4)]
        tail[v] = jnp.where(
            lane < 64, jnp.where(lane < 32, s[0], s[1]), jnp.where(lane < 96, s[2], s[3])
        )

    def windows_one(v, n):
        parts = [jnp.concatenate([taps[2 * (v + t) + k] for t in range(n)], 0) for k in range(6)]
        parts += [tail[pl.ds(v + d, n)].reshape(n * 32, 128) for d in (0, 2)]
        return jnp.concatenate(parts, axis=1)

    def windows_two(ref, q, n):
        parts = [
            jnp.concatenate([ref[i, 2 * (q + t) + k] for t in range(n)], 0)
            for i in range(3)
            for k in range(4)
        ]
        return jnp.concatenate(parts, axis=1)

    def first(m, carry):
        v = m * ONE
        pre = jnp.dot(windows_one(v, ONE), w1[...], preferred_element_type=F32)
        for r in range(2):
            h, s = gelu_and_slope(pre[:, r * 128 : r * 128 + 128].reshape(ONE, 32, 128))
            at = (pl.ds(v, ONE), slice(r * 32, r * 32 + 32))
            slope[at] = s
            for i, copy in enumerate(row_copies(h)):
                hid[(i,) + at] = copy
        return carry

    lax.fori_loop(0, 66 // ONE, first, 0, unroll=True)

    @pl.when(place[0] == 0)
    def _():
        hid[:, 0] = jnp.zeros((3, 64, 128), BF)
        slope[0] = jnp.zeros((64, 128), F32)

    @pl.when(place[1] == 0)
    def _():
        hid[:, 65] = jnp.zeros((3, 64, 128), BF)
        slope[65] = jnp.zeros((64, 128), F32)

    delta[:, 0:2] = jnp.zeros((3, 2, 64, 128), BF)
    delta[:, 66:68] = jnp.zeros((3, 2, 64, 128), BF)

    def second(m, carry):
        q = m * TWO
        pre = jnp.dot(windows_two(hid, q, TWO), w2[...], preferred_element_type=F32)
        for s in range(2):
            f, sl = gelu_and_slope(pre[:, s * 128 : s * 128 + 128].reshape(TWO, 64, 128))
            fmap[pl.ds(q, TWO), s] = f.astype(BF)
            d = cot[pl.ds(q, TWO), s].astype(F32) * sl
            pairs2[pl.ds(q, TWO), :, s * 128 : s * 128 + 128] = d.astype(BF)
            for i, copy in enumerate(reversed(row_copies(d.reshape(TWO * 2, 32, 128)))):
                copy = copy.reshape(TWO, 64, 128)
                for t in range(TWO):
                    delta[i, 2 * (q + t) + 2 + s] = copy[t]
        return carry

    lax.fori_loop(0, 32 // TWO, second, 0, unroll=True)
    acc2[...] = over_rows(pairs2[...].reshape(2048, 256), windows_two(hid, 0, 32))

    def back(m, carry):
        q = m * BACK
        both = jnp.dot(windows_two(delta, q, BACK), wb[...], preferred_element_type=F32)
        for s in range(2):
            b = both[:, s * 128 : s * 128 + 128].reshape(BACK, 64, 128)
            for t in range(BACK):
                v = 2 * (q + t) + s
                d = (b[t] * slope[v]).astype(BF)
                pairs1[v, :, 0:128] = d[0:32]
                pairs1[v, :, 128:256] = d[32:64]
        return carry

    lax.fori_loop(0, 33 // BACK, back, 0, unroll=True)
    acc1[...] = over_rows(pairs1[...].reshape(2112, 256), windows_one(0, 66))

    for i in range(3):
        for j in range(3):
            at = (i * 4 + j) * 128
            to = (i * 3 + j) * 128
            both = acc2[0:128, at : at + 128] + acc2[128:256, at + 128 : at + 256]
            total[to : to + 128] = both.T
    for j in range(5):
        at = j * 128
        both = (acc1[0:128, at : at + 128] + acc1[128:256, at + 128 : at + 256]).T
        for i in range(4):
            to = 1152 + (i * 5 + j) * 32
            total[to : to + 32] = both[i * 32 : i * 32 + 32]
    even = acc1[0:128, 768:1024].T
    odd = acc1[128:256, 768:1024].T
    total[1792:1952] = even[0:160] + odd[32:192]
    total[1952:2048] = jnp.zeros((96, 128), F32)
    mine = pl.multiple_of(place[2] * 1024, 1024)
    other = pl.multiple_of((1 - place[2]) * 1024, 1024)
    keep[...] = total[pl.ds(mine, 1024)]
    send[...] = total[pl.ds(other, 1024)].astype(BF)


def block(place, low, middle, high, w1, w2, wb, cot):
    vmem = pl.BlockSpec(memory_space=pltpu.VMEM)
    return pl.pallas_call(
        block_kernel,
        out_shape=(
            jax.ShapeDtypeStruct((32, 2, 64, 128), BF),
            jax.ShapeDtypeStruct((1024, 128), F32),
            jax.ShapeDtypeStruct((1024, 128), BF),
        ),
        in_specs=[pl.BlockSpec(memory_space=pltpu.SMEM)] + [vmem] * 7,
        out_specs=(vmem, vmem, vmem),
        scratch_shapes=[
            pltpu.VMEM((136, 32, 128), BF),
            pltpu.VMEM((140, 32, 128), BF),
            pltpu.VMEM((68, 32, 128), BF),
            pltpu.VMEM((3, 66, 64, 128), BF),
            pltpu.VMEM((66, 64, 128), F32),
            pltpu.VMEM((3, 68, 64, 128), BF),
            pltpu.VMEM((32, 64, 256), BF),
            pltpu.VMEM((66, 32, 256), BF),
            pltpu.VMEM((256, 1536), F32),
            pltpu.VMEM((256, 1024), F32),
            pltpu.VMEM((2048, 128), F32),
        ],
        compiler_params=pltpu.CompilerParams(vmem_limit_bytes=45 * 1024 * 1024),
        cost_estimate=pl.CostEstimate(
            flops=5_500_000_000, bytes_accessed=5_000_000, transcendentals=1_100_000
        ),
    )(place, low, middle, high, w1, w2, wb, cot.reshape(32, 2, 64, 128))


def columns_first(block_of):
    return jnp.transpose(block_of[0], (2, 1, 0))


def fourfold(v):
    return jnp.tile(v, (1, 1, 4))


TRACK = ("y", "zh")
REP = ("x", "zl", "core")


def exchange(pieces, axes):
    return lax.all_to_all(pieces, axes, 0, 0, tiled=True)


def gathered(piece, axes, count):
    return exchange(jnp.broadcast_to(piece[None], (count,) + piece.shape), axes)


def summed(pieces):
    return jnp.sum(pieces.astype(F32), axis=0).astype(BF)


def on_device(features, kernel_one, kernel_two, cotangent):
    at = lax.axis_index(TRACK)
    core = lax.axis_index("core")
    up = [(i, i + 1) for i in range(15)]
    down = [(i + 1, i) for i in range(15)]
    middle = lax.optimization_barrier(fourfold(columns_first(features)))
    low = lax.ppermute(middle[124:], TRACK, up)
    high = lax.ppermute(middle[:4], TRACK, down)
    place = jnp.stack([(at > 0).astype(jnp.int32), (at < 15).astype(jnp.int32), core])
    cot = columns_first(cotangent)
    fmap, keep, send = block(place, low, middle, high, *weights(kernel_one, kernel_two), cot)
    swap = [(0, 1), (1, 0)]
    sibling = lax.ppermute(send, "core", swap)
    feature_map = jnp.transpose(fmap.reshape(128, 32, 128), (2, 1, 0))[None]
    chip_sum = (keep + sibling.astype(F32)).astype(BF)
    layer_sum = summed(exchange(chip_sum.reshape(16, 64, 128), ("x", "y")))
    full_sum = summed(gathered(layer_sum, ("zh", "zl"), 8))
    half = gathered(full_sum, ("x", "y"), 16).reshape(1024, 128)
    rest = lax.ppermute(half, "core", swap)
    rows = jnp.concatenate(
        [jnp.where(core == 0, half, rest), jnp.where(core == 0, rest, half)], axis=0
    ).astype(F32)
    grad_two = rows[:1152].reshape(3, 3, 128, 128)
    grad_one = rows[1152:1952].reshape(5, 5, 32, 128)
    return (feature_map, grad_one, grad_two)


def solution(mesh):
    fine = Mesh(mesh.devices.reshape(4, 4, 4, 2, 2), TRACK + REP)
    placed = (P(REP, None, None, TRACK), P(), P(), P(REP, None, None, TRACK))
    return jax.shard_map(
        on_device,
        mesh=fine,
        in_specs=placed,
        out_specs=(P(REP, None, None, TRACK), P(), P()),
        check_vma=False,
    )
```

```python
import jax
import jax.numpy as jnp
from jax import lax
from jax.experimental import pallas as pl
from jax.experimental.pallas import tpu as pltpu
from jax.sharding import Mesh, PartitionSpec as P

scale_a = 0.7978845608
scale_b = 0.044715
BF = jnp.bfloat16
F32 = jnp.float32
ONE = 6
TWO = 2
BACK = 3


def gelu_and_slope(v):
    c = (scale_a * scale_b) * (v * v)
    t = jnp.tanh(v * (scale_a + c))
    p = 0.5 + 0.5 * t
    value = v * p
    slope = p + value * (scale_a + 3.0 * c) * (1.0 - t)
    return value, slope


def shifted(v, shift):
    rows = v.shape[1]
    h = lax.broadcasted_iota(jnp.int32, v.shape, 1)
    rolled = pltpu.roll(v, (-shift) % rows, 1)
    keep = (h < rows - shift) if shift > 0 else (h >= -shift)
    return jnp.where(keep, rolled, jnp.zeros_like(rolled))


def row_copies(v):
    v = v.astype(BF)
    z = jnp.zeros((v.shape[0], 2, v.shape[2]), BF)
    return jnp.concatenate([z, v[:, :-2]], axis=1), v, jnp.concatenate([v[:, 2:], z], axis=1)


def over_rows(a, b):
    return lax.dot_general(a, b, (((0,), (0,)), ((), ())), preferred_element_type=F32)


def weights_kernel(k1, k2, w1, w2, wb):
    zero = jnp.zeros((32, 128), BF)
    for k in range(6):
        for r in range(2):
            j = k - r
            for i in range(5):
                row = k * 128 + i * 32 if i < 4 else 768 + k * 32
                w1[row : row + 32, r * 128 : r * 128 + 128] = k1[i, j] if 0 <= j < 5 else zero
    w1[960:1024] = jnp.zeros((64, 256), BF)
    square = jnp.zeros((128, 128), BF)
    for i in range(3):
        for s in range(2):
            lanes = slice(s * 128, s * 128 + 128)
            for k in range(4):
                rows = slice((i * 4 + k) * 128, (i * 4 + k) * 128 + 128)
                j = k - s
                w2[rows, lanes] = k2[i, j] if 0 <= j < 3 else square
                j = s + 2 - k
                wb[rows, lanes] = k2[i, j].T if 0 <= j < 3 else square


def weights(k1, k2):
    vmem = pl.BlockSpec(memory_space=pltpu.VMEM)
    return pl.pallas_call(
        weights_kernel,
        out_shape=(
            jax.ShapeDtypeStruct((1024, 256), BF),
            jax.ShapeDtypeStruct((1536, 256), BF),
            jax.ShapeDtypeStruct((1536, 256), BF),
        ),
        in_specs=[vmem] * 2,
        out_specs=(vmem,) * 3,
        compiler_params=pltpu.CompilerParams(vmem_limit_bytes=8 * 1024 * 1024),
        cost_estimate=pl.CostEstimate(flops=0, bytes_accessed=2_500_000, transcendentals=0),
    )(k1, k2)


def block_kernel(
    place, low, middle, high, w1, w2, wb, cot, fmap, keep, send,
    taps, bottom, tail, hid, slope, delta, pairs2, pairs1, acc2, acc1, total,
):
    bottom[136:140] = jnp.zeros((4, 32, 128), BF)
    lane = lax.broadcasted_iota(jnp.int32, (4, 32, 128), 2)
    for n in range(34):
        at = slice(n * 4, n * 4 + 4)
        x = low[...] if n == 0 else high[...] if n == 33 else middle[n * 4 - 4 : n * 4]
        v = x.astype(F32)
        taps[at] = jnp.where(
            lane < 64,
            jnp.where(lane < 32, shifted(v, -2), shifted(v, -1)),
            jnp.where(lane < 96, v, shifted(v, 1)),
        ).astype(BF)
        bottom[at] = row_copies(x)[2]
    lane = lax.broadcasted_iota(jnp.int32, (32, 128), 1)
    for v in range(68):
        s = [bottom[2 * v + k] for k in range(4)]
        tail[v] = jnp.where(
            lane < 64, jnp.where(lane < 32, s[0], s[1]), jnp.where(lane < 96, s[2], s[3])
        )

    def windows_one(v, n):
        parts = [jnp.concatenate([taps[2 * (v + t) + k] for t in range(n)], 0) for k in range(6)]
        parts += [tail[pl.ds(v + d, n)].reshape(n * 32, 128) for d in (0, 2)]
        return jnp.concatenate(parts, axis=1)

    def windows_two(ref, q, n):
        parts = [
            jnp.concatenate([ref[i, 2 * (q + t) + k] for t in range(n)], 0)
            for i in range(3)
            for k in range(4)
        ]
        return jnp.concatenate(parts, axis=1)

    def first(m, carry):
        v = m * ONE
        pre = jnp.dot(windows_one(v, ONE), w1[...], preferred_element_type=F32)
        for r in range(2):
            h, s = gelu_and_slope(pre[:, r * 128 : r * 128 + 128].reshape(ONE, 32, 128))
            at = (pl.ds(v, ONE), slice(r * 32, r * 32 + 32))
            slope[at] = s
            for i, copy in enumerate(row_copies(h)):
                hid[(i,) + at] = copy
        return carry

    lax.fori_loop(0, 66 // ONE, first, 0, unroll=True)

    @pl.when(place[0] == 0)
    def _():
        hid[:, 0] = jnp.zeros((3, 64, 128), BF)
        slope[0] = jnp.zeros((64, 128), F32)

    @pl.when(place[1] == 0)
    def _():
        hid[:, 65] = jnp.zeros((3, 64, 128), BF)
        slope[65] = jnp.zeros((64, 128), F32)

    delta[:, 0:2] = jnp.zeros((3, 2, 64, 128), BF)
    delta[:, 66:68] = jnp.zeros((3, 2, 64, 128), BF)

    def second(m, carry):
        q = m * TWO
        pre = jnp.dot(windows_two(hid, q, TWO), w2[...], preferred_element_type=F32)
        for s in range(2):
            f, sl = gelu_and_slope(pre[:, s * 128 : s * 128 + 128].reshape(TWO, 64, 128))
            fmap[pl.ds(q, TWO), s] = f.astype(BF)
            d = cot[pl.ds(q, TWO), s].astype(F32) * sl
            pairs2[pl.ds(q, TWO), :, s * 128 : s * 128 + 128] = d.astype(BF)
            for i, copy in enumerate(reversed(row_copies(d.reshape(TWO * 2, 32, 128)))):
                copy = copy.reshape(TWO, 64, 128)
                for t in range(TWO):
                    delta[i, 2 * (q + t) + 2 + s] = copy[t]
        return carry

    lax.fori_loop(0, 32 // TWO, second, 0, unroll=True)
    acc2[...] = over_rows(pairs2[...].reshape(2048, 256), windows_two(hid, 0, 32))

    def back(m, carry):
        q = m * BACK
        both = jnp.dot(windows_two(delta, q, BACK), wb[...], preferred_element_type=F32)
        for s in range(2):
            b = both[:, s * 128 : s * 128 + 128].reshape(BACK, 64, 128)
            for t in range(BACK):
                v = 2 * (q + t) + s
                d = (b[t] * slope[v]).astype(BF)
                pairs1[v, :, 0:128] = d[0:32]
                pairs1[v, :, 128:256] = d[32:64]
        return carry

    lax.fori_loop(0, 33 // BACK, back, 0, unroll=True)
    acc1[...] = over_rows(pairs1[...].reshape(2112, 256), windows_one(0, 66))

    for i in range(3):
        for j in range(3):
            at = (i * 4 + j) * 128
            to = (i * 3 + j) * 128
            both = acc2[0:128, at : at + 128] + acc2[128:256, at + 128 : at + 256]
            total[to : to + 128] = both.T
    for j in range(5):
        at = j * 128
        both = (acc1[0:128, at : at + 128] + acc1[128:256, at + 128 : at + 256]).T
        for i in range(4):
            to = 1152 + (i * 5 + j) * 32
            total[to : to + 32] = both[i * 32 : i * 32 + 32]
    even = acc1[0:128, 768:1024].T
    odd = acc1[128:256, 768:1024].T
    total[1792:1952] = even[0:160] + odd[32:192]
    total[1952:2048] = jnp.zeros((96, 128), F32)
    mine = pl.multiple_of(place[2] * 1024, 1024)
    other = pl.multiple_of((1 - place[2]) * 1024, 1024)
    keep[...] = total[pl.ds(mine, 1024)].astype(BF)
    send[...] = total[pl.ds(other, 1024)].astype(BF)


def half_kernel(core, half, *refs):
    grad_two, grad_one, wide, left = refs[-4:]
    wide[...] = half[...].astype(F32)

    @pl.when(core[0] == 0)
    def _():
        copy = pltpu.make_async_copy(wide, grad_two.at[pl.ds(0, 1024)], left.at[0])
        copy.start()
        copy.wait()

    @pl.when(core[0] != 0)
    def _():
        two = pltpu.make_async_copy(
            wide.at[pl.ds(0, 128)], grad_two.at[pl.ds(1024, 128)], left.at[0]
        )
        one = pltpu.make_async_copy(wide.at[pl.ds(128, 800)], grad_one, left.at[1])
        two.start()
        one.start()
        two.wait()
        one.wait()


def write_half(core, half, *grads):
    anywhere = pl.BlockSpec(memory_space=pl.ANY)
    return pl.pallas_call(
        half_kernel,
        out_shape=(
            jax.ShapeDtypeStruct((1152, 128), F32),
            jax.ShapeDtypeStruct((800, 128), F32),
        ),
        in_specs=[
            pl.BlockSpec(memory_space=pltpu.SMEM),
            pl.BlockSpec(memory_space=pltpu.VMEM),
        ]
        + [anywhere] * len(grads),
        out_specs=(anywhere, anywhere),
        scratch_shapes=[pltpu.VMEM((1024, 128), F32), pltpu.SemaphoreType.DMA((2,))],
        input_output_aliases={2: 0, 3: 1} if grads else {},
        compiler_params=pltpu.CompilerParams(vmem_limit_bytes=8 * 1024 * 1024),
        cost_estimate=pl.CostEstimate(flops=0, bytes_accessed=1_500_000, transcendentals=0),
    )(core, half, *grads)


def block(place, low, middle, high, w1, w2, wb, cot):
    vmem = pl.BlockSpec(memory_space=pltpu.VMEM)
    return pl.pallas_call(
        block_kernel,
        out_shape=(
            jax.ShapeDtypeStruct((32, 2, 64, 128), BF),
            jax.ShapeDtypeStruct((1024, 128), BF),
            jax.ShapeDtypeStruct((1024, 128), BF),
        ),
        in_specs=[pl.BlockSpec(memory_space=pltpu.SMEM)] + [vmem] * 7,
        out_specs=(vmem, vmem, vmem),
        scratch_shapes=[
            pltpu.VMEM((136, 32, 128), BF),
            pltpu.VMEM((140, 32, 128), BF),
            pltpu.VMEM((68, 32, 128), BF),
            pltpu.VMEM((3, 66, 64, 128), BF),
            pltpu.VMEM((66, 64, 128), F32),
            pltpu.VMEM((3, 68, 64, 128), BF),
            pltpu.VMEM((32, 64, 256), BF),
            pltpu.VMEM((66, 32, 256), BF),
            pltpu.VMEM((256, 1536), F32),
            pltpu.VMEM((256, 1024), F32),
            pltpu.VMEM((2048, 128), F32),
        ],
        compiler_params=pltpu.CompilerParams(vmem_limit_bytes=45 * 1024 * 1024),
        cost_estimate=pl.CostEstimate(
            flops=5_500_000_000, bytes_accessed=5_000_000, transcendentals=1_100_000
        ),
    )(place, low, middle, high, w1, w2, wb, cot.reshape(32, 2, 64, 128))


def columns_first(block_of):
    return jnp.transpose(block_of[0], (2, 1, 0))


def fourfold(v):
    return jnp.tile(v, (1, 1, 4))


TRACK = ("y", "zh")
REP = ("x", "zl", "core")


def exchange(pieces, axes):
    return lax.all_to_all(pieces, axes, 0, 0, tiled=True)


def gathered(piece, axes, count):
    return exchange(jnp.broadcast_to(piece[None], (count,) + piece.shape), axes)


def summed(pieces):
    return jnp.sum(pieces.astype(F32), axis=0).astype(BF)


def on_device(features, kernel_one, kernel_two, cotangent):
    at = lax.axis_index(TRACK)
    core = lax.axis_index("core")
    up = [(i, i + 1) for i in range(15)]
    down = [(i + 1, i) for i in range(15)]
    middle = lax.optimization_barrier(fourfold(columns_first(features)))
    low = lax.ppermute(middle[124:], TRACK, up)
    high = lax.ppermute(middle[:4], TRACK, down)
    place = jnp.stack([(at > 0).astype(jnp.int32), (at < 15).astype(jnp.int32), core])
    cot = columns_first(cotangent)
    fmap, keep, send = block(place, low, middle, high, *weights(kernel_one, kernel_two), cot)
    swap = [(0, 1), (1, 0)]
    sibling = lax.ppermute(send, "core", swap)
    feature_map = jnp.transpose(fmap.reshape(128, 32, 128), (2, 1, 0))[None]
    sibling, feature_map = lax.optimization_barrier((sibling, feature_map))
    chip_sum = (keep.astype(F32) + sibling.astype(F32)).astype(BF)
    layer_sum = summed(exchange(chip_sum.reshape(16, 64, 128), ("x", "y")))
    full_sum = summed(gathered(layer_sum, ("zh", "zl"), 8))
    half = gathered(full_sum, ("x", "y"), 16).reshape(1024, 128)
    rest = lax.ppermute(half, "core", swap)
    grads = write_half(core[None], half)
    grad_two, grad_one = write_half(1 - core[None], rest, *grads)
    return (feature_map, grad_one.reshape(5, 5, 32, 128), grad_two.reshape(3, 3, 128, 128))


def solution(mesh):
    fine = Mesh(mesh.devices.reshape(4, 4, 4, 2, 2), TRACK + REP)
    placed = (P(REP, None, None, TRACK), P(), P(), P(REP, None, None, TRACK))
    return jax.shard_map(
        on_device,
        mesh=fine,
        in_specs=placed,
        out_specs=(P(REP, None, None, TRACK), P(), P()),
        check_vma=False,
    )
```
